32 devices in a mesh: ep: 8 (over z, y), sp: 4 (over x, core).
Axes of the slice: x: 2, y: 2, z: 4, core: 2. Of those that a mesh axis runs over, the one named last changes fastest.
Arguments:
- stream: bfloat16 [4096, 4096], P(('ep', 'sp')), may hold values from -30 to 30
- query_base: bfloat16 [4096, 4096], P(('ep', 'sp')), may hold values from -40 to 40
- key_heads: bfloat16 [4096, 1024], P(('ep', 'sp')), may hold values from -6 to 6
- value_heads: bfloat16 [4096, 1024], P(('ep', 'sp')), may hold values from -12 to 12
- attention_gain: bfloat16 [4096], replicated, may hold values from 0.099609375 to 1.8984375
- expert_gain: bfloat16 [4096], replicated, may hold values from 0.099609375 to 1.8984375
- adapter_down: bfloat16 [4096, 128], P('sp'), may hold values from -0.09375 to 0.09375
- adapter_up: bfloat16 [4096, 128], P('sp'), may hold values from -1 to 1
- user_index: int32 [8], P('ep'), may hold values from 0 to 3
- routes: int32 [4096, 2], P('ep'), may hold values from 0 to 7, all different within a row; in each aligned block of 128 rows (0 to 127, 128 to 255, ...) at most 40 rows name the same one
- route_weights: int32 [4096, 2], P(('ep', 'sp')), may hold values from 1 to 4
- gate_weight: bfloat16 [8, 4096, 1536], P('ep', None, 'sp'), may hold values from -0.09375 to 0.09375
- up_weight: bfloat16 [8, 4096, 1536], P('ep', None, 'sp'), may hold values from -0.09375 to 0.09375
- down_weight: bfloat16 [8, 1536, 4096], P('ep', 'sp'), may hold values from -0.15625 to 0.15625
Outputs:
- hidden_state: bfloat16 [4096, 4096], P(('ep', 'sp'))
- moe_out: bfloat16 [4096, 4096], P(('ep', 'sp'))
The draws below stay inside these ranges and needn't reach their ends.
Inputs may be any that keep to these rules, and one draw needn't show every extreme that they name: `routes`: each row names 2 different experts. In each aligned block of 128 rows (the tokens of one device) no expert is named more than 40 times, and in some block some expert is named exactly 40 times.
All inputs are finite; a program needn't handle non-finite values.
Results may differ from the reference program's by a relative error of at most 0.019.
Values may be sent and summed in bfloat16 or wider, within the bound.
A program may use at most 128 MiB of HBM per device.

```python
import math
import jax
import jax.numpy as jnp
import numpy as np
from jax import lax

D = 4096
HEADS = 32
KV_HEADS = 8
HEAD = 128
FF = 1536
USERS = 4
RANK = 32
TOP = 2
TOK_DEV = 128
SEQ_LEN = 512
SEQS = 8
TOKENS = 4096
EXPERTS = 8
CAP = 40
N_SP = 4


def key_field(key):
    base_key = jax.random.fold_in(key, 101)
    field_rows = jnp.clip(jax.random.normal(base_key, (TOKENS, KV_HEADS * HEAD), jnp.float32), -6.0, 6.0)
    return field_rows


def draw_key_heads(key, part):
    return key_field(key).astype(jnp.bfloat16)


def draw_query_base(key, part):
    base_key = jax.random.fold_in(key, 201)
    base_rows = jnp.clip(jax.random.normal(base_key, (TOKENS, D), jnp.float32), -6.0, 6.0)
    return base_rows.astype(jnp.bfloat16)


def draw_stream(key, part):
    base_key = jax.random.fold_in(key, 301)
    field_rows = jnp.clip(jax.random.normal(base_key, (TOKENS, D), jnp.float32), -6.0, 6.0)
    return field_rows.astype(jnp.bfloat16)


def set_ends(array, stream_key, low, high):
    shape = array.shape
    index_at = [jax.random.randint(jax.random.fold_in(stream_key, axis), (), 0, shape[axis]) for axis in range(len(shape))]
    array = array.at[tuple(index_at)].set(low)
    longest = shape.index(max(shape))
    index_at[longest] = (index_at[longest] + 1) % shape[longest]
    return array.at[tuple(index_at)].set(high)


def shard_levels(key, shape, split, smallest, top_value):
    factor_of, own = 1.0, jax.random.fold_in(key, 6)
    for dim, blocks in split:
        heights = jnp.exp(jax.random.uniform(jax.random.fold_in(own, dim), (blocks,), jnp.float32, smallest / len(split), top_value / len(split)))
        factor_of = factor_of * jnp.repeat(heights, shape[dim] // blocks).reshape([-1 if axis == dim else 1 for axis in range(len(shape))])
    return factor_of


def assign_block(own_key, own, number, rows, amount, top, most, skew):
    ranking = jax.random.permutation(own_key, amount)
    crowded, usual = portions_of(amount, rows * top, most, skew, True), portions_of(amount, rows * top, most, skew, False)
    places = jnp.arange(amount)

    def named(sizes, turn):
        used = int((sizes > 0).sum())
        fixed = max(1, used // 4)
        passed = fixed + (places - fixed + turn * (used - fixed)) % max(1, amount - fixed)
        return jnp.zeros((amount,), jnp.int32).at[ranking[jnp.where(places < fixed, places, passed)]].set(jnp.asarray(sizes, jnp.int32))

    sizes = jnp.where(number % 4 == 0, named(crowded, number // 4), named(usual, number - number // 4 - 1))
    mixed = jax.random.permutation(jax.random.fold_in(own, 3), amount)
    donor, sink = mixed[0:amount // 2 * 2:2], mixed[1:amount // 2 * 2:2]
    room = jnp.minimum(sizes[donor] - 1, most - sizes[sink]) // 2
    room = jnp.where((donor == ranking[0]) | (sink == ranking[0]) | (sizes[sink] == 0), 0, jnp.maximum(room, 0))
    passed = jax.random.randint(jax.random.fold_in(own, 4), (amount // 2,), 0, 1 << 20) % (room + 1)
    sizes = sizes.at[donor].add(-passed).at[sink].add(passed)
    members = jnp.searchsorted(jnp.cumsum(sizes), jnp.arange(rows * top), side="right").astype(jnp.int32)
    grid = members.reshape(top, rows).T
    grid = grid[jax.random.permutation(jax.random.fold_in(own, 1), rows)]
    turn = jax.random.randint(jax.random.fold_in(own, 2), (rows, 1), 0, top)
    return jnp.take_along_axis(grid, (jnp.arange(top)[None, :] + turn) % top, axis=1)


def portions_of(amount, total, most, slope, full):
    weights = [(1 << 20) // math.isqrt(rank ** slope) + 1 for rank in range(1, amount + 1)]
    largest = most if full else min(most, max(-(-total // amount), total * weights[0] // sum(weights)))
    least = 1 if total - largest >= amount - 1 else 0
    holding, spare = [largest] + [least] * (amount - 1), total - largest - least * (amount - 1)
    while spare > 0:
        free = [i for i in range(1, amount) if holding[i] < largest] or [i for i in range(1, amount) if holding[i] < most]
        whole, left = sum([weights[i] for i in free]), spare
        for i in free:
            more = min(most - holding[i], max(1, left * weights[i] // whole), spare)
            holding[i] = holding[i] + more
            spare = spare - more
    return np.array(holding)


def scatter_about(rng, shape, deviation, most, pieces=(), held_as=jnp.bfloat16):
    factor_of = shard_levels(rng, shape, pieces, -0.22, 0.18) if pieces else 1.0
    entries = jax.random.normal(rng, shape, jnp.float32) * deviation * factor_of
    return jnp.minimum(jnp.maximum(entries, -most), most).astype(held_as)


def setup_inputs(seed: int = 0) -> dict:
    streams_of = jax.random.split(jax.random.key(seed), 15)
    stream = draw_stream(jax.random.fold_in(streams_of[14], 71), 0)
    query_base = draw_query_base(jax.random.fold_in(streams_of[14], 71), 0)
    key_heads = draw_key_heads(jax.random.fold_in(streams_of[14], 71), 0)
    value_heads = scatter_about(streams_of[3], (TOKENS, KV_HEADS * HEAD), 2.0, 12.0, ((0, 32),))
    attention_gain = jnp.clip(1.0 + 0.18 * jax.random.normal(streams_of[4], (D,), jnp.float32), 0.099609375, 1.8984375).astype(jnp.bfloat16)
    expert_gain = jnp.clip(1.0 + 0.18 * jax.random.normal(streams_of[5], (D,), jnp.float32), 0.099609375, 1.8984375).astype(jnp.bfloat16)
    adapter_down = scatter_about(streams_of[6], (D, USERS * RANK), D ** -0.5, 0.09375, ((0, 4),))
    adapter_up = scatter_about(streams_of[7], (D, USERS * RANK), RANK ** -0.5, 1.0, ((0, 4),))
    user_index = set_ends(jax.random.randint(streams_of[8], (SEQS,), 0, USERS), jax.random.fold_in(streams_of[8], 1), 0, USERS - 1).astype(jnp.int32)
    routes_keys = jax.random.split(jax.random.fold_in(streams_of[9], 1), TOKENS // TOK_DEV)
    routes_turns = jax.random.permutation(jax.random.fold_in(streams_of[9], 3), TOKENS // TOK_DEV)
    routes = jax.vmap(lambda own, number: assign_block(jax.random.fold_in(streams_of[9], 2), own, number, TOK_DEV, EXPERTS, TOP, CAP, 2))(routes_keys, routes_turns).reshape((TOKENS, TOP))
    route_weights = set_ends(jax.random.randint(streams_of[10], (TOKENS, TOP), 1, 5), jax.random.fold_in(streams_of[10], 1), 1, 4).astype(jnp.int32)
    gate_weight = scatter_about(streams_of[11], (EXPERTS, D, FF), D ** -0.5, 0.09375, ((0, 8), (2, 4)))
    up_weight = scatter_about(streams_of[12], (EXPERTS, D, FF), D ** -0.5, 0.09375, ((0, 8), (2, 4)))
    down_weight = scatter_about(streams_of[13], (EXPERTS, FF, D), FF ** -0.5, 0.15625, ((0, 8), (1, 4)))
    return dict(stream=stream, query_base=query_base, key_heads=key_heads, value_heads=value_heads, attention_gain=attention_gain, expert_gain=expert_gain, adapter_down=adapter_down, adapter_up=adapter_up, user_index=user_index, routes=routes, route_weights=route_weights, gate_weight=gate_weight, up_weight=up_weight, down_weight=down_weight)


epsilon = 1e-06

def rms_scale(inputs, gain_vec):
    widened = inputs.astype(jnp.float32)
    return widened * lax.rsqrt(lax.optimization_barrier(jnp.mean(widened * widened, axis=-1, keepdims=True)) + epsilon) * gain_vec.astype(jnp.float32)

def route_slots(block_routes, experts):
    flat_routes = block_routes.reshape(-1)
    matches = (flat_routes[:, None] == jnp.arange(experts, dtype=jnp.int32)[None, :]).astype(jnp.int32)
    earlier = jnp.cumsum(matches, axis=0) - matches
    return (flat_routes, lax.optimization_barrier(jnp.sum(earlier * matches, axis=1)).astype(jnp.int32))

def attention_block(stream_rows, base_rows, key_rows, value_rows, user_id, attention_gain, adapter_down, adapter_up):
    normed = rms_scale(stream_rows, attention_gain).astype(jnp.bfloat16)
    down_cols = lax.dynamic_slice_in_dim(adapter_down, (user_id * RANK).astype(jnp.int32), RANK, 1)
    up_cols = lax.dynamic_slice_in_dim(adapter_up, (user_id * RANK).astype(jnp.int32), RANK, 1)
    low_rank = jnp.dot(normed, down_cols, preferred_element_type=jnp.float32).astype(jnp.bfloat16)
    adapter_delta = jnp.dot(low_rank, up_cols.T, preferred_element_type=jnp.float32)
    queries = (base_rows.astype(jnp.float32) + adapter_delta).astype(jnp.bfloat16)
    group_size = HEADS // KV_HEADS
    row_total = queries.shape[0]
    query_heads = queries.reshape(row_total, KV_HEADS, group_size, HEAD).astype(jnp.float32)
    key_split = key_rows.reshape(-1, KV_HEADS, HEAD).astype(jnp.float32)
    value_split = value_rows.reshape(-1, KV_HEADS, HEAD).astype(jnp.float32)
    scores = jnp.einsum('qhgd,khd->hgqk', query_heads, key_split) * HEAD ** (-0.5)
    row_max = lax.optimization_barrier(jnp.max(scores, axis=-1, keepdims=True))
    exponent = jnp.exp(scores - row_max)
    attn_probs = (exponent / lax.optimization_barrier(jnp.sum(exponent, axis=-1, keepdims=True))).astype(jnp.bfloat16)
    attended = jnp.einsum('hgqk,khd->qhgd', attn_probs.astype(jnp.float32), value_split).reshape(row_total, D)
    return (stream_rows.astype(jnp.float32) + attended).astype(jnp.bfloat16)

def reference(stream, query_base, key_heads, value_heads, attention_gain, expert_gain, adapter_down, adapter_up, user_index, routes, route_weights, gate_weight, up_weight, down_weight):

    def per_sequence(packed):
        stream_rows, base_rows, key_rows, value_rows, user_id = packed
        return attention_block(stream_rows, base_rows, key_rows, value_rows, user_id, attention_gain, adapter_down, adapter_up)
    hidden_state = lax.map(per_sequence, (stream.reshape(SEQS, SEQ_LEN, D), query_base.reshape(SEQS, SEQ_LEN, D), key_heads.reshape(SEQS, SEQ_LEN, -1), value_heads.reshape(SEQS, SEQ_LEN, -1), user_index)).reshape(TOKENS, D)
    normed_moe = rms_scale(hidden_state, expert_gain).astype(jnp.bfloat16)
    weights = route_weights.astype(jnp.float32)
    weights = weights / lax.optimization_barrier(jnp.sum(weights, axis=1, keepdims=True))
    blocks = TOKENS // TOK_DEV
    flat_all, slot_all = jax.vmap(lambda block_rows: route_slots(block_rows, EXPERTS))(routes.reshape(blocks, TOK_DEV, TOP))
    block_ids = jnp.broadcast_to(jnp.arange(blocks, dtype=jnp.int32)[:, None], flat_all.shape)
    token_ids = block_ids * TOK_DEV + jnp.arange(TOK_DEV * TOP, dtype=jnp.int32)[None, :] // TOP
    slot_table = jnp.full((EXPERTS, blocks, CAP), TOKENS, jnp.int32).at[flat_all, block_ids, slot_all].set(token_ids)
    share_table = jnp.zeros((EXPERTS, blocks, CAP), jnp.float32).at[flat_all, block_ids, slot_all].set(weights.reshape(blocks, -1))
    padded = jnp.concatenate([normed_moe, jnp.zeros((1, D), jnp.bfloat16)], axis=0)

    def expert_step(total, packed):
        index_rows, share_rows, gate_one, up_one, down_one = packed
        rows_in = padded[index_rows]
        gate_out = jnp.dot(rows_in, gate_one, preferred_element_type=jnp.float32)
        up_out = jnp.dot(rows_in, up_one, preferred_element_type=jnp.float32)
        activated = (jax.nn.silu(gate_out) * up_out).astype(jnp.bfloat16)
        parts = jnp.einsum('mjf,jfd->jmd', activated.reshape(-1, N_SP, FF // N_SP).astype(jnp.float32), down_one.reshape(N_SP, FF // N_SP, D).astype(jnp.float32)).astype(jnp.bfloat16)
        expert_out = lax.optimization_barrier(jnp.sum(parts.astype(jnp.float32), axis=0)).astype(jnp.bfloat16)
        total = total.at[index_rows].add(share_rows[:, None] * expert_out.astype(jnp.float32))
        return (total, None)
    total, unused = lax.scan(expert_step, jnp.zeros((TOKENS + 1, D), jnp.float32), (slot_table.reshape(EXPERTS, -1), share_table.reshape(EXPERTS, -1), gate_weight, up_weight, down_weight))
    moe_out = total[:TOKENS].astype(jnp.bfloat16)
    return (hidden_state, moe_out)
```

```python
import jax
import jax.numpy as jnp
from jax import lax
from jax.experimental import pallas as pl
from jax.experimental.pallas import tpu as pltpu
from jax.sharding import PartitionSpec as P

D = 4096
HEADS = 32
KV_HEADS = 8
HEAD = 128
RANK = 32


epsilon = 1e-06


def rms_scale(inputs, gain_vec):
    widened = inputs.astype(jnp.float32)
    return (
        widened
        * lax.rsqrt(jnp.mean(widened * widened, axis=-1, keepdims=True) + epsilon)
        * gain_vec.astype(jnp.float32)
    )


def route_slots(block_routes, experts):
    flat_routes = block_routes.reshape(-1)
    matches = (flat_routes[:, None] == jnp.arange(experts, dtype=jnp.int32)[None, :]).astype(
        jnp.int32
    )
    earlier = jnp.cumsum(matches, axis=0) - matches
    return (flat_routes, jnp.sum(earlier * matches, axis=1))


def attention_block(
    stream_rows, base_rows, key_rows, value_rows, attention_gain, down_cols, up_cols
):
    normed = rms_scale(stream_rows, attention_gain).astype(jnp.bfloat16)
    low_rank = lax.dot_general(
        normed, down_cols, (((1,), (1,)), ((), ())), preferred_element_type=jnp.float32
    ).astype(jnp.bfloat16)
    adapter_delta = jnp.dot(low_rank, up_cols, preferred_element_type=jnp.float32)
    queries = (base_rows.astype(jnp.float32) + adapter_delta).astype(jnp.bfloat16)
    group_size = HEADS // KV_HEADS
    row_total = queries.shape[0]
    query_heads = queries.reshape(row_total, KV_HEADS, group_size, HEAD)
    key_split = key_rows.reshape(-1, KV_HEADS, HEAD)
    value_split = value_rows.reshape(-1, KV_HEADS, HEAD)
    scores = jnp.einsum(
        "qhgd,khd->hgqk", query_heads, key_split, preferred_element_type=jnp.float32
    ) * HEAD ** (-0.5)
    row_max = jnp.max(scores, axis=-1, keepdims=True)
    exponent = jnp.exp(scores - row_max)
    attn_probs = (exponent / jnp.sum(exponent, axis=-1, keepdims=True)).astype(jnp.bfloat16)
    attended = jnp.einsum(
        "hgqk,khd->qhgd", attn_probs, value_split, preferred_element_type=jnp.float32
    ).reshape(row_total, D)
    return (stream_rows.astype(jnp.float32) + attended).astype(jnp.bfloat16)


STEPS = 8


def peer_mask(step):
    return (step * 2) % STEPS + step // 4


def xor3(a, b):
    total = 0
    for place in (1, 2, 4):
        abit, bbit = (a // place) % 2, (b // place) % 2
        total = total + place * (abit + bbit - 2 * abit * bbit)
    return total


def expert_kernel(
    outgoing,
    gate_hbm,
    up_hbm,
    down_hbm,
    returned,
    arrived,
    part,
    from_core,
    from_x,
    rows_in,
    gate_w,
    up_w,
    down_w,
    weight_sem,
    send_sem,
    recv_sem,
):
    me, sp = lax.axis_index("ep"), lax.axis_index("sp")
    xpos, core = sp // 2, sp % 2
    core_dev, x_dev = xpos * 2 + (1 - core), (1 - xpos) * 2 + core
    q_me, q_core = core * 2 + xpos, (1 - core) * 2 + xpos
    q_x, q_diag = core * 2 + (1 - xpos), (1 - core) * 2 + (1 - xpos)
    cap, width = outgoing.shape[1], outgoing.shape[2]
    Z, C1, X, C2, RC, RX, FIN = range(7)

    def remote(kind, step, src, dst, ep_dev, sp_dev):
        return pltpu.make_async_remote_copy(
            src_ref=src,
            dst_ref=dst,
            send_sem=send_sem.at[kind, step],
            recv_sem=recv_sem.at[kind, step],
            device_id=(ep_dev, sp_dev),
            device_id_type=pl.DeviceIdType.MESH,
        )

    def peer(step):
        return xor3(me, peer_mask(step))

    def z_send(k):
        return remote(Z, k, outgoing.at[k], arrived.at[k, q_me], peer(k), sp)

    def core_send(k):
        return remote(C1, k, arrived.at[k, q_me], arrived.at[k, q_me], me, core_dev)

    def x_send(k):
        return remote(X, k, arrived.at[k, q_me], arrived.at[k, q_me], me, x_dev)

    def core_forward(k):
        return remote(C2, k, arrived.at[k, q_x], arrived.at[k, q_x], me, core_dev)

    def part_send(k):
        return remote(RC, k, part.at[k, pl.ds((1 - core) * 2, 2)], from_core.at[k], me, core_dev)

    def x_part_send(k):
        return remote(RX, k, part.at[k, q_x], from_x.at[k], me, x_dev)

    def final_send(k):
        return remote(FIN, k, part.at[k, q_me], returned.at[k], peer(k), sp)

    weights = [
        pltpu.make_async_copy(src, dst, weight_sem.at[n])
        for n, (src, dst) in enumerate(((gate_hbm, gate_w), (up_hbm, up_w), (down_hbm, down_w)))
    ]
    for copy in weights:
        copy.start()
    barrier = pltpu.get_barrier_semaphore()
    for step in range(1, STEPS):
        pl.semaphore_signal(
            barrier, inc=1, device_id=(peer(step), sp), device_id_type=pl.DeviceIdType.MESH
        )
    for near in (core_dev, x_dev):
        pl.semaphore_signal(
            barrier, inc=1, device_id=(me, near), device_id_type=pl.DeviceIdType.MESH
        )
    pl.semaphore_wait(barrier, STEPS + 1)

    for step in range(1, STEPS):
        z_send(step).start()
    arrived[0, q_me] = outgoing[0]

    def compute(k):
        chunk = 512
        for col in range(0, width, chunk):
            cols = slice(col, col + chunk)
            rows_in[:, cols] = jnp.concatenate(
                [arrived[k, q, :, cols].astype(jnp.float32) for q in range(4)], axis=0
            ).astype(jnp.bfloat16)
        rows = rows_in[...]
        gate = jnp.dot(rows, gate_w[...], preferred_element_type=jnp.float32)
        up = jnp.dot(rows, up_w[...], preferred_element_type=jnp.float32)
        act = (gate / (1.0 + jnp.exp(-gate)) * up).astype(jnp.bfloat16)
        for col in range(0, width, chunk):
            cols = slice(col, col + chunk)
            out = jnp.dot(act, down_w[:, cols], preferred_element_type=jnp.float32)
            for q in range(4):
                part[k, q, :, cols] = out[q * cap : (q + 1) * cap].astype(jnp.bfloat16)

    def body(t, carry):
        @pl.when(t < STEPS)
        def _():
            @pl.when(t > 0)
            def _():
                remote(Z, t, outgoing.at[t], arrived.at[t, q_me], peer(t), sp).wait_recv()

            x_send(t).start()
            core_send(t).start()

        @pl.when((t >= 1) & (t < STEPS + 1))
        def _():
            k = t - 1
            remote(X, k, arrived.at[k, q_x], arrived.at[k, q_x], me, x_dev).wait_recv()
            core_forward(k).start()

        @pl.when(t == 2)
        def _():
            for copy in weights:
                copy.wait()

        @pl.when((t >= 2) & (t < STEPS + 2))
        def _():
            k = t - 2
            remote(C1, k, arrived.at[k, q_core], arrived.at[k, q_core], me, core_dev).wait_recv()
            remote(C2, k, arrived.at[k, q_diag], arrived.at[k, q_diag], me, core_dev).wait_recv()
            compute(k)
            part_send(k).start()

        @pl.when((t >= 3) & (t < STEPS + 3))
        def _():
            k = t - 3
            part_send(k).wait_recv()
            part[k, q_x] = (
                part[k, q_x].astype(jnp.float32)
                + from_core[k, 1 - xpos].astype(jnp.float32)
            ).astype(jnp.bfloat16)
            x_part_send(k).start()

        @pl.when(t >= 4)
        def _():
            k = t - 4
            x_part_send(k).wait_recv()
            part[k, q_me] = (
                part[k, q_me].astype(jnp.float32)
                + from_core[k, xpos].astype(jnp.float32)
                + from_x[k].astype(jnp.float32)
            ).astype(jnp.bfloat16)

            @pl.when(k > 0)
            def _():
                final_send(k).start()

        return carry

    lax.fori_loop(0, STEPS + 4, body, 0)
    returned[0] = part[0, q_me]
    for k in range(STEPS):
        if k > 0:
            z_send(k).wait_send()
            final_send(k).wait()
        for copy in (core_send, x_send, core_forward, part_send, x_part_send):
            copy(k).wait_send()


def expert_exchange(outgoing, gate_local, up_local, down_local):
    steps, cap, width = outgoing.shape
    hidden = gate_local.shape[1]
    rows = 4 * steps * cap
    dma = pltpu.SemaphoreType.DMA
    return pl.pallas_call(
        expert_kernel,
        out_shape=jax.ShapeDtypeStruct(outgoing.shape, jnp.bfloat16),
        in_specs=[pl.BlockSpec(memory_space=pltpu.VMEM)] + [pl.BlockSpec(memory_space=pl.ANY)] * 3,
        out_specs=pl.BlockSpec(memory_space=pltpu.VMEM),
        scratch_shapes=[
            pltpu.VMEM((steps, 4, cap, width), jnp.bfloat16),
            pltpu.VMEM((steps, 4, cap, width), jnp.bfloat16),
            pltpu.VMEM((steps, 2, cap, width), jnp.bfloat16),
            pltpu.VMEM((steps, cap, width), jnp.bfloat16),
            pltpu.VMEM((4 * cap, width), jnp.bfloat16),
            pltpu.VMEM(gate_local.shape, jnp.bfloat16),
            pltpu.VMEM(up_local.shape, jnp.bfloat16),
            pltpu.VMEM(down_local.shape, jnp.bfloat16),
            dma((3,)),
            dma((7, steps)),
            dma((7, steps)),
        ],
        compiler_params=pltpu.CompilerParams(
            collective_id=0, has_side_effects=True, vmem_limit_bytes=60 * 1024 * 1024
        ),
        cost_estimate=pl.CostEstimate(
            flops=6 * rows * width * hidden, bytes_accessed=8 * rows * width, transcendentals=0
        ),
    )(outgoing, gate_local, up_local, down_local)


def expert_collectives(outgoing, gate_local, up_local, down_local):
    experts, capacity, model_width = outgoing.shape
    received = lax.all_to_all(outgoing, "ep", split_axis=0, concat_axis=0, tiled=True)
    all_rows = lax.all_gather(received, "sp", axis=0, tiled=True).reshape(-1, model_width)
    gate_out = jnp.dot(all_rows, gate_local, preferred_element_type=jnp.float32)
    up_out = jnp.dot(all_rows, up_local, preferred_element_type=jnp.float32)
    activated = (jax.nn.silu(gate_out) * up_out).astype(jnp.bfloat16)
    summed = lax.psum_scatter(
        jnp.dot(activated, down_local, preferred_element_type=jnp.float32).astype(jnp.bfloat16),
        "sp",
        scatter_dimension=0,
        tiled=True,
    )
    expert_out = summed.reshape(experts, capacity, model_width)
    return lax.all_to_all(expert_out, "ep", split_axis=0, concat_axis=0, tiled=True)


def on_device(
    stream,
    query_base,
    key_heads,
    value_heads,
    attention_gain,
    expert_gain,
    adapter_down,
    adapter_up,
    user_index,
    routes,
    route_weights,
    gate_weight,
    up_weight,
    down_weight,
):
    user_id = user_index[0]
    tokens_dev, model_width = stream.shape
    down_cols = lax.dynamic_slice_in_dim(adapter_down, user_id * RANK, RANK, 1).T
    up_cols = lax.dynamic_slice_in_dim(adapter_up, user_id * RANK, RANK, 1).T
    shared = jnp.concatenate([key_heads, value_heads, down_cols, up_cols], axis=0)
    shared = lax.all_gather(shared, "sp", axis=0, tiled=False)
    key_all = shared[:, :tokens_dev].reshape(-1, key_heads.shape[1])
    value_all = shared[:, tokens_dev : 2 * tokens_dev].reshape(-1, value_heads.shape[1])
    adapters = shared[:, 2 * tokens_dev :].transpose(1, 0, 2).reshape(2 * RANK, model_width)
    hidden_state = attention_block(
        stream, query_base, key_all, value_all, attention_gain, adapters[:RANK], adapters[RANK:]
    )
    normed_moe = rms_scale(hidden_state, expert_gain).astype(jnp.bfloat16)
    top_count = routes.shape[1]
    experts = lax.axis_size("ep")
    capacity = max(2, (5 * tokens_dev * top_count + 4 * experts - 1) // (4 * experts))
    own_routes = lax.dynamic_slice_in_dim(routes, lax.axis_index("sp") * tokens_dev, tokens_dev, 0)
    in_kernel = experts == STEPS and capacity % 8 == 0 and lax.axis_size("sp") == 4
    flat_routes, slot_index = route_slots(own_routes, experts)
    if in_kernel:
        mask = flat_routes ^ lax.axis_index("ep")
        flat_routes = mask // 2 + (mask % 2) * 4
    position = (flat_routes * capacity + slot_index).reshape(tokens_dev, top_count)
    slots = jnp.arange(experts * capacity, dtype=jnp.int32)
    chosen = position[:, :, None] == slots
    placed = jnp.any(chosen, axis=1).astype(jnp.bfloat16)
    outgoing = (
        lax.dot_general(
            placed, normed_moe, (((0,), (0,)), ((), ())), preferred_element_type=jnp.float32
        )
        .astype(jnp.bfloat16)
        .reshape(experts, capacity, model_width)
    )
    exchange = expert_exchange if in_kernel else expert_collectives
    returned = exchange(outgoing, gate_weight[0], up_weight[0], down_weight[0])
    returned = returned.reshape(experts * capacity, model_width)
    route_share = route_weights.astype(jnp.float32)
    route_share = route_share / jnp.sum(route_share, axis=1, keepdims=True)
    moe_out = sum(
        jnp.dot(
            chosen[:, k].astype(jnp.bfloat16), returned, preferred_element_type=jnp.float32
        )
        * route_share[:, k : k + 1]
        for k in range(top_count)
    ).astype(jnp.bfloat16)
    return (hidden_state, moe_out)


def solution(mesh):
    in_specs = (
        P(("ep", "sp"), None),
        P(("ep", "sp"), None),
        P(("ep", "sp"), None),
        P(("ep", "sp"), None),
        P(),
        P(),
        P("sp", None),
        P("sp", None),
        P("ep"),
        P("ep", None),
        P(("ep", "sp"), None),
        P("ep", None, "sp"),
        P("ep", None, "sp"),
        P("ep", "sp", None),
    )
    out_specs = (P(("ep", "sp"), None), P(("ep", "sp"), None))
    return jax.shard_map(
        on_device, mesh=mesh, in_specs=in_specs, out_specs=out_specs, check_vma=False
    )
```

```python
import jax
import jax.numpy as jnp
from jax import lax
from jax.experimental import pallas as pl
from jax.experimental.pallas import tpu as pltpu
from jax.sharding import PartitionSpec as P

D = 4096
HEADS = 32
KV_HEADS = 8
HEAD = 128
RANK = 32


epsilon = 1e-06


def rms_scale(inputs, gain_vec):
    widened = inputs.astype(jnp.float32)
    return (
        widened
        * lax.rsqrt(jnp.mean(widened * widened, axis=-1, keepdims=True) + epsilon)
        * gain_vec.astype(jnp.float32)
    )


def route_slots(block_routes, experts):
    flat_routes = block_routes.reshape(-1)
    matches = (flat_routes[:, None] == jnp.arange(experts, dtype=jnp.int32)[None, :]).astype(
        jnp.int32
    )
    earlier = jnp.cumsum(matches, axis=0) - matches
    return (flat_routes, jnp.sum(earlier * matches, axis=1))


def attention_block(
    stream_rows, base_rows, key_rows, value_rows, attention_gain, down_cols, up_cols
):
    normed = rms_scale(stream_rows, attention_gain).astype(jnp.bfloat16)
    low_rank = lax.dot_general(
        normed, down_cols, (((1,), (1,)), ((), ())), preferred_element_type=jnp.float32
    ).astype(jnp.bfloat16)
    adapter_delta = jnp.dot(low_rank, up_cols, preferred_element_type=jnp.float32)
    queries = (base_rows.astype(jnp.float32) + adapter_delta).astype(jnp.bfloat16)
    group_size = HEADS // KV_HEADS
    row_total = queries.shape[0]
    query_heads = queries.reshape(row_total, KV_HEADS, group_size, HEAD)
    key_split = key_rows.reshape(-1, KV_HEADS, HEAD)
    value_split = value_rows.reshape(-1, KV_HEADS, HEAD)
    scores = jnp.einsum(
        "qhgd,khd->hgqk", query_heads, key_split, preferred_element_type=jnp.float32
    ) * HEAD ** (-0.5)
    row_max = jnp.max(scores, axis=-1, keepdims=True)
    exponent = jnp.exp(scores - row_max)
    attn_probs = (exponent / jnp.sum(exponent, axis=-1, keepdims=True)).astype(jnp.bfloat16)
    attended = jnp.einsum(
        "hgqk,khd->qhgd", attn_probs, value_split, preferred_element_type=jnp.float32
    ).reshape(row_total, D)
    return (stream_rows.astype(jnp.float32) + attended).astype(jnp.bfloat16)


STEPS = 8
AHEAD = 4


def peer_mask(step):
    return (step * 2) % STEPS + step // 4


def xor3(a, b):
    total = 0
    for place in (1, 2, 4):
        abit, bbit = (a // place) % 2, (b // place) % 2
        total = total + place * (abit + bbit - 2 * abit * bbit)
    return total


def expert_kernel(
    outgoing,
    gate_hbm,
    up_hbm,
    down_hbm,
    returned,
    arrived,
    part,
    from_core,
    from_x,
    rows_in,
    gate_w,
    up_w,
    down_w,
    weight_sem,
    send_sem,
    recv_sem,
):
    me, sp = lax.axis_index("ep"), lax.axis_index("sp")
    xpos, core = sp // 2, sp % 2
    core_dev, x_dev = xpos * 2 + (1 - core), (1 - xpos) * 2 + core
    q_me, q_core = core * 2 + xpos, (1 - core) * 2 + xpos
    q_x, q_diag = core * 2 + (1 - xpos), (1 - core) * 2 + (1 - xpos)
    cap, width = outgoing.shape[1], outgoing.shape[2]
    Z, C1, X, C2, RC, RX, FIN = range(7)

    def remote(kind, step, src, dst, ep_dev, sp_dev):
        return pltpu.make_async_remote_copy(
            src_ref=src,
            dst_ref=dst,
            send_sem=send_sem.at[kind, step],
            recv_sem=recv_sem.at[kind, step],
            device_id=(ep_dev, sp_dev),
            device_id_type=pl.DeviceIdType.MESH,
        )

    def peer(step):
        return xor3(me, peer_mask(step))

    def z_send(k):
        return remote(Z, k, outgoing.at[k], arrived.at[k, q_me], peer(k), sp)

    def core_send(k):
        return remote(C1, k, arrived.at[k, q_me], arrived.at[k, q_me], me, core_dev)

    def x_send(k):
        return remote(X, k, arrived.at[k, q_me], arrived.at[k, q_me], me, x_dev)

    def core_forward(k):
        return remote(C2, k, arrived.at[k, q_x], arrived.at[k, q_x], me, core_dev)

    def part_send(k):
        return remote(RC, k, part.at[k, pl.ds((1 - core) * 2, 2)], from_core.at[k], me, core_dev)

    def x_part_send(k):
        return remote(RX, k, part.at[k, q_x], from_x.at[k], me, x_dev)

    def final_send(k):
        return remote(FIN, k, part.at[k, q_me], returned.at[k], peer(k), sp)

    weights = [
        pltpu.make_async_copy(src, dst, weight_sem.at[n])
        for n, (src, dst) in enumerate(((gate_hbm, gate_w), (up_hbm, up_w), (down_hbm, down_w)))
    ]
    for copy in weights:
        copy.start()
    barrier = pltpu.get_barrier_semaphore()
    for step in range(1, STEPS):
        pl.semaphore_signal(
            barrier, inc=1, device_id=(peer(step), sp), device_id_type=pl.DeviceIdType.MESH
        )
    for near in (core_dev, x_dev):
        pl.semaphore_signal(
            barrier, inc=1, device_id=(me, near), device_id_type=pl.DeviceIdType.MESH
        )
    pl.semaphore_wait(barrier, STEPS + 1)

    for step in range(1, AHEAD + 1):
        z_send(step).start()
    arrived[0, q_me] = outgoing[0]

    def compute(k):
        chunk = 512
        for col in range(0, width, chunk):
            cols = slice(col, col + chunk)
            rows_in[:, cols] = jnp.concatenate(
                [arrived[k, q, :, cols].astype(jnp.float32) for q in range(4)], axis=0
            ).astype(jnp.bfloat16)
        rows = rows_in[...]
        gate = jnp.dot(rows, gate_w[...], preferred_element_type=jnp.float32)
        up = jnp.dot(rows, up_w[...], preferred_element_type=jnp.float32)
        act = (gate / (1.0 + jnp.exp(-gate)) * up).astype(jnp.bfloat16)
        for col in range(0, width, chunk):
            cols = slice(col, col + chunk)
            out = jnp.dot(act, down_w[:, cols], preferred_element_type=jnp.float32)
            for q in range(4):
                part[k, q, :, cols] = out[q * cap : (q + 1) * cap].astype(jnp.bfloat16)

    def body(t, carry):
        @pl.when(t < STEPS)
        def _():
            @pl.when(t > 0)
            def _():
                remote(Z, t, outgoing.at[t], arrived.at[t, q_me], peer(t), sp).wait_recv()

                @pl.when(t < STEPS - AHEAD)
                def _():
                    z_send(t + AHEAD).start()

            x_send(t).start()
            core_send(t).start()

        @pl.when((t >= 1) & (t < STEPS + 1))
        def _():
            k = t - 1
            remote(X, k, arrived.at[k, q_x], arrived.at[k, q_x], me, x_dev).wait_recv()
            core_forward(k).start()

        @pl.when((t >= 2) & (t < STEPS + 2))
        def _():
            k = t - 2
            part_send(k).wait_recv()
            part[k, q_x] = (
                part[k, q_x].astype(jnp.float32)
                + from_core[k, 1 - xpos].astype(jnp.float32)
            ).astype(jnp.bfloat16)
            x_part_send(k).start()

        @pl.when(t >= 3)
        def _():
            k = t - 3
            x_part_send(k).wait_recv()
            part[k, q_me] = (
                part[k, q_me].astype(jnp.float32)
                + from_core[k, xpos].astype(jnp.float32)
                + from_x[k].astype(jnp.float32)
            ).astype(jnp.bfloat16)

            @pl.when(k > 0)
            def _():
                final_send(k).start()

        @pl.when(t == 1)
        def _():
            for copy in weights:
                copy.wait()

        @pl.when((t >= 1) & (t < STEPS + 1))
        def _():
            k = t - 1
            remote(C1, k, arrived.at[k, q_core], arrived.at[k, q_core], me, core_dev).wait_recv()
            remote(C2, k, arrived.at[k, q_diag], arrived.at[k, q_diag], me, core_dev).wait_recv()
            compute(k)
            part_send(k).start()

        return carry

    lax.fori_loop(0, STEPS + 3, body, 0)
    returned[0] = part[0, q_me]
    for k in range(STEPS):
        if k > 0:
            z_send(k).wait_send()
            final_send(k).wait()
        for copy in (core_send, x_send, core_forward, part_send, x_part_send):
            copy(k).wait_send()


def expert_exchange(outgoing, gate_local, up_local, down_local):
    steps, cap, width = outgoing.shape
    hidden = gate_local.shape[1]
    rows = 4 * steps * cap
    dma = pltpu.SemaphoreType.DMA
    return pl.pallas_call(
        expert_kernel,
        out_shape=jax.ShapeDtypeStruct(outgoing.shape, jnp.bfloat16),
        in_specs=[pl.BlockSpec(memory_space=pltpu.VMEM)] + [pl.BlockSpec(memory_space=pl.ANY)] * 3,
        out_specs=pl.BlockSpec(memory_space=pltpu.VMEM),
        scratch_shapes=[
            pltpu.VMEM((steps, 4, cap, width), jnp.bfloat16),
            pltpu.VMEM((steps, 4, cap, width), jnp.bfloat16),
            pltpu.VMEM((steps, 2, cap, width), jnp.bfloat16),
            pltpu.VMEM((steps, cap, width), jnp.bfloat16),
            pltpu.VMEM((4 * cap, width), jnp.bfloat16),
            pltpu.VMEM(gate_local.shape, jnp.bfloat16),
            pltpu.VMEM(up_local.shape, jnp.bfloat16),
            pltpu.VMEM(down_local.shape, jnp.bfloat16),
            dma((3,)),
            dma((7, steps)),
            dma((7, steps)),
        ],
        compiler_params=pltpu.CompilerParams(
            collective_id=0, has_side_effects=True, vmem_limit_bytes=60 * 1024 * 1024
        ),
        cost_estimate=pl.CostEstimate(
            flops=6 * rows * width * hidden, bytes_accessed=8 * rows * width, transcendentals=0
        ),
    )(outgoing, gate_local, up_local, down_local)


def expert_collectives(outgoing, gate_local, up_local, down_local):
    experts, capacity, model_width = outgoing.shape
    received = lax.all_to_all(outgoing, "ep", split_axis=0, concat_axis=0, tiled=True)
    all_rows = lax.all_gather(received, "sp", axis=0, tiled=True).reshape(-1, model_width)
    gate_out = jnp.dot(all_rows, gate_local, preferred_element_type=jnp.float32)
    up_out = jnp.dot(all_rows, up_local, preferred_element_type=jnp.float32)
    activated = (jax.nn.silu(gate_out) * up_out).astype(jnp.bfloat16)
    summed = lax.psum_scatter(
        jnp.dot(activated, down_local, preferred_element_type=jnp.float32).astype(jnp.bfloat16),
        "sp",
        scatter_dimension=0,
        tiled=True,
    )
    expert_out = summed.reshape(experts, capacity, model_width)
    return lax.all_to_all(expert_out, "ep", split_axis=0, concat_axis=0, tiled=True)


def on_device(
    stream,
    query_base,
    key_heads,
    value_heads,
    attention_gain,
    expert_gain,
    adapter_down,
    adapter_up,
    user_index,
    routes,
    route_weights,
    gate_weight,
    up_weight,
    down_weight,
):
    user_id = user_index[0]
    tokens_dev, model_width = stream.shape
    down_cols = lax.dynamic_slice_in_dim(adapter_down, user_id * RANK, RANK, 1).T
    up_cols = lax.dynamic_slice_in_dim(adapter_up, user_id * RANK, RANK, 1).T
    shared = jnp.concatenate([key_heads, value_heads, down_cols, up_cols], axis=0)
    shared = lax.all_gather(shared, "sp", axis=0, tiled=False)
    key_all = shared[:, :tokens_dev].reshape(-1, key_heads.shape[1])
    value_all = shared[:, tokens_dev : 2 * tokens_dev].reshape(-1, value_heads.shape[1])
    adapters = shared[:, 2 * tokens_dev :].transpose(1, 0, 2).reshape(2 * RANK, model_width)
    hidden_state = attention_block(
        stream, query_base, key_all, value_all, attention_gain, adapters[:RANK], adapters[RANK:]
    )
    normed_moe = rms_scale(hidden_state, expert_gain).astype(jnp.bfloat16)
    top_count = routes.shape[1]
    experts = lax.axis_size("ep")
    capacity = max(2, (5 * tokens_dev * top_count + 4 * experts - 1) // (4 * experts))
    own_routes = lax.dynamic_slice_in_dim(routes, lax.axis_index("sp") * tokens_dev, tokens_dev, 0)
    in_kernel = experts == STEPS and capacity % 8 == 0 and lax.axis_size("sp") == 4
    flat_routes, slot_index = route_slots(own_routes, experts)
    if in_kernel:
        mask = flat_routes ^ lax.axis_index("ep")
        flat_routes = mask // 2 + (mask % 2) * 4
    position = (flat_routes * capacity + slot_index).reshape(tokens_dev, top_count)
    slots = jnp.arange(experts * capacity, dtype=jnp.int32)
    chosen = position[:, :, None] == slots
    placed = jnp.any(chosen, axis=1).astype(jnp.bfloat16)
    outgoing = (
        lax.dot_general(
            placed, normed_moe, (((0,), (0,)), ((), ())), preferred_element_type=jnp.float32
        )
        .astype(jnp.bfloat16)
        .reshape(experts, capacity, model_width)
    )
    exchange = expert_exchange if in_kernel else expert_collectives
    returned = exchange(outgoing, gate_weight[0], up_weight[0], down_weight[0])
    returned = returned.reshape(experts * capacity, model_width)
    route_share = route_weights.astype(jnp.float32)
    route_share = route_share / jnp.sum(route_share, axis=1, keepdims=True)
    moe_out = sum(
        jnp.dot(
            chosen[:, k].astype(jnp.bfloat16), returned, preferred_element_type=jnp.float32
        )
        * route_share[:, k : k + 1]
        for k in range(top_count)
    ).astype(jnp.bfloat16)
    return (hidden_state, moe_out)


def solution(mesh):
    in_specs = (
        P(("ep", "sp"), None),
        P(("ep", "sp"), None),
        P(("ep", "sp"), None),
        P(("ep", "sp"), None),
        P(),
        P(),
        P("sp", None),
        P("sp", None),
        P("ep"),
        P("ep", None),
        P(("ep", "sp"), None),
        P("ep", None, "sp"),
        P("ep", None, "sp"),
        P("ep", "sp", None),
    )
    out_specs = (P(("ep", "sp"), None), P(("ep", "sp"), None))
    return jax.shard_map(
        on_device, mesh=mesh, in_specs=in_specs, out_specs=out_specs, check_vma=False
    )
```

```python
import jax
import jax.numpy as jnp
from jax import lax
from jax.experimental import pallas as pl
from jax.experimental.pallas import tpu as pltpu
from jax.sharding import PartitionSpec as P

D = 4096
HEADS = 32
KV_HEADS = 8
HEAD = 128
RANK = 32


epsilon = 1e-06


def rms_scale(inputs, gain_vec):
    widened = inputs.astype(jnp.float32)
    return (
        widened
        * lax.rsqrt(jnp.mean(widened * widened, axis=-1, keepdims=True) + epsilon)
        * gain_vec.astype(jnp.float32)
    )


def route_slots(block_routes, experts):
    flat_routes = block_routes.reshape(-1)
    matches = (flat_routes[:, None] == jnp.arange(experts, dtype=jnp.int32)[None, :]).astype(
        jnp.int32
    )
    earlier = jnp.cumsum(matches, axis=0) - matches
    return (flat_routes, jnp.sum(earlier * matches, axis=1))


def attention_block(
    stream_rows, base_rows, key_rows, value_rows, attention_gain, down_cols, up_cols
):
    normed = rms_scale(stream_rows, attention_gain).astype(jnp.bfloat16)
    low_rank = lax.dot_general(
        normed, down_cols, (((1,), (1,)), ((), ())), preferred_element_type=jnp.float32
    ).astype(jnp.bfloat16)
    adapter_delta = jnp.dot(low_rank, up_cols, preferred_element_type=jnp.float32)
    queries = (base_rows.astype(jnp.float32) + adapter_delta).astype(jnp.bfloat16)
    group_size = HEADS // KV_HEADS
    row_total = queries.shape[0]
    query_heads = queries.reshape(row_total, KV_HEADS, group_size, HEAD)
    key_split = key_rows.reshape(-1, KV_HEADS, HEAD)
    value_split = value_rows.reshape(-1, KV_HEADS, HEAD)
    scores = jnp.einsum(
        "qhgd,khd->hgqk", query_heads, key_split, preferred_element_type=jnp.float32
    ) * HEAD ** (-0.5)
    row_max = jnp.max(scores, axis=-1, keepdims=True)
    exponent = jnp.exp(scores - row_max)
    attn_probs = (exponent / jnp.sum(exponent, axis=-1, keepdims=True)).astype(jnp.bfloat16)
    attended = jnp.einsum(
        "hgqk,khd->qhgd", attn_probs, value_split, preferred_element_type=jnp.float32
    ).reshape(row_total, D)
    return (stream_rows.astype(jnp.float32) + attended).astype(jnp.bfloat16)


STEPS = 8
AHEAD = 4


def peer_mask(step):
    middle, last = (step // 2) % 2, step // 4
    return step % 2 + 2 * last + 4 * ((middle + last) % 2)


def xor3(a, b):
    total = 0
    for place in (1, 2, 4):
        abit, bbit = (a // place) % 2, (b // place) % 2
        total = total + place * (abit + bbit - 2 * abit * bbit)
    return total


def expert_kernel(
    outgoing,
    gate_hbm,
    up_hbm,
    down_hbm,
    returned,
    arrived,
    part,
    from_core,
    from_x,
    rows_in,
    gate_w,
    up_w,
    down_w,
    weight_sem,
    send_sem,
    recv_sem,
):
    me, sp = lax.axis_index("ep"), lax.axis_index("sp")
    xpos, core = sp // 2, sp % 2
    core_dev, x_dev = xpos * 2 + (1 - core), (1 - xpos) * 2 + core
    q_me, q_core = core * 2 + xpos, (1 - core) * 2 + xpos
    q_x, q_diag = core * 2 + (1 - xpos), (1 - core) * 2 + (1 - xpos)
    cap, width = outgoing.shape[1], outgoing.shape[2]
    Z, C1, X, C2, RC, RX, FIN = range(7)

    def remote(kind, step, src, dst, ep_dev, sp_dev):
        return pltpu.make_async_remote_copy(
            src_ref=src,
            dst_ref=dst,
            send_sem=send_sem.at[kind, step],
            recv_sem=recv_sem.at[kind, step],
            device_id=(ep_dev, sp_dev),
            device_id_type=pl.DeviceIdType.MESH,
        )

    def peer(step):
        return xor3(me, peer_mask(step))

    def z_send(k):
        return remote(Z, k, outgoing.at[k], arrived.at[k, q_me], peer(k), sp)

    def core_send(k):
        return remote(C1, k, arrived.at[k, q_me], arrived.at[k, q_me], me, core_dev)

    def x_send(k):
        return remote(X, k, arrived.at[k, q_me], arrived.at[k, q_me], me, x_dev)

    def core_forward(k):
        return remote(C2, k, arrived.at[k, q_x], arrived.at[k, q_x], me, core_dev)

    def part_send(k):
        return remote(RC, k, part.at[k, pl.ds((1 - core) * 2, 2)], from_core.at[k], me, core_dev)

    def x_part_send(k):
        return remote(RX, k, part.at[k, q_x], from_x.at[k], me, x_dev)

    def final_send(k):
        return remote(FIN, k, part.at[k, q_me], returned.at[k], peer(k), sp)

    weights = [
        pltpu.make_async_copy(src, dst, weight_sem.at[n])
        for n, (src, dst) in enumerate(((gate_hbm, gate_w), (up_hbm, up_w), (down_hbm, down_w)))
    ]
    for copy in weights:
        copy.start()
    barrier = pltpu.get_barrier_semaphore()
    for step in range(1, STEPS):
        pl.semaphore_signal(
            barrier, inc=1, device_id=(peer(step), sp), device_id_type=pl.DeviceIdType.MESH
        )
    for near in (core_dev, x_dev):
        pl.semaphore_signal(
            barrier, inc=1, device_id=(me, near), device_id_type=pl.DeviceIdType.MESH
        )
    pl.semaphore_wait(barrier, STEPS + 1)

    for step in range(1, AHEAD + 1):
        z_send(step).start()
    arrived[0, q_me] = outgoing[0]

    def compute(k):
        chunk = 512
        for col in range(0, width, chunk):
            cols = slice(col, col + chunk)
            rows_in[:, cols] = jnp.concatenate(
                [arrived[k, q, :, cols].astype(jnp.float32) for q in range(4)], axis=0
            ).astype(jnp.bfloat16)
        rows = rows_in[...]
        gate = jnp.dot(rows, gate_w[...], preferred_element_type=jnp.float32)
        up = jnp.dot(rows, up_w[...], preferred_element_type=jnp.float32)
        act = (gate / (1.0 + jnp.exp(-gate)) * up).astype(jnp.bfloat16)
        for col in range(0, width, chunk):
            cols = slice(col, col + chunk)
            out = jnp.dot(act, down_w[:, cols], preferred_element_type=jnp.float32)
            for q in range(4):
                part[k, q, :, cols] = out[q * cap : (q + 1) * cap].astype(jnp.bfloat16)

    def body(t, carry):
        @pl.when(t < STEPS)
        def _():
            @pl.when(t > 0)
            def _():
                remote(Z, t, outgoing.at[t], arrived.at[t, q_me], peer(t), sp).wait_recv()

                @pl.when(t < STEPS - AHEAD)
                def _():
                    z_send(t + AHEAD).start()

            x_send(t).start()
            core_send(t).start()

        @pl.when((t >= 1) & (t < STEPS + 1))
        def _():
            k = t - 1
            remote(X, k, arrived.at[k, q_x], arrived.at[k, q_x], me, x_dev).wait_recv()
            core_forward(k).start()

        @pl.when((t >= 2) & (t < STEPS + 2))
        def _():
            k = t - 2
            part_send(k).wait_recv()
            part[k, q_x] = (
                part[k, q_x].astype(jnp.float32)
                + from_core[k, 1 - xpos].astype(jnp.float32)
            ).astype(jnp.bfloat16)
            x_part_send(k).start()

        @pl.when(t >= 3)
        def _():
            k = t - 3
            x_part_send(k).wait_recv()
            part[k, q_me] = (
                part[k, q_me].astype(jnp.float32)
                + from_core[k, xpos].astype(jnp.float32)
                + from_x[k].astype(jnp.float32)
            ).astype(jnp.bfloat16)

            @pl.when(k > 0)
            def _():
                final_send(k).start()

        @pl.when(t == 1)
        def _():
            for copy in weights:
                copy.wait()

        @pl.when((t >= 1) & (t < STEPS + 1))
        def _():
            k = t - 1
            remote(C1, k, arrived.at[k, q_core], arrived.at[k, q_core], me, core_dev).wait_recv()
            remote(C2, k, arrived.at[k, q_diag], arrived.at[k, q_diag], me, core_dev).wait_recv()
            compute(k)
            part_send(k).start()

        return carry

    lax.fori_loop(0, STEPS + 3, body, 0)
    returned[0] = part[0, q_me]
    for k in range(STEPS):
        if k > 0:
            z_send(k).wait_send()
            final_send(k).wait()
        for copy in (core_send, x_send, core_forward, part_send, x_part_send):
            copy(k).wait_send()


def expert_exchange(outgoing, gate_local, up_local, down_local):
    steps, cap, width = outgoing.shape
    hidden = gate_local.shape[1]
    rows = 4 * steps * cap
    dma = pltpu.SemaphoreType.DMA
    return pl.pallas_call(
        expert_kernel,
        out_shape=jax.ShapeDtypeStruct(outgoing.shape, jnp.bfloat16),
        in_specs=[pl.BlockSpec(memory_space=pltpu.VMEM)] + [pl.BlockSpec(memory_space=pl.ANY)] * 3,
        out_specs=pl.BlockSpec(memory_space=pltpu.VMEM),
        scratch_shapes=[
            pltpu.VMEM((steps, 4, cap, width), jnp.bfloat16),
            pltpu.VMEM((steps, 4, cap, width), jnp.bfloat16),
            pltpu.VMEM((steps, 2, cap, width), jnp.bfloat16),
            pltpu.VMEM((steps, cap, width), jnp.bfloat16),
            pltpu.VMEM((4 * cap, width), jnp.bfloat16),
            pltpu.VMEM(gate_local.shape, jnp.bfloat16),
            pltpu.VMEM(up_local.shape, jnp.bfloat16),
            pltpu.VMEM(down_local.shape, jnp.bfloat16),
            dma((3,)),
            dma((7, steps)),
            dma((7, steps)),
        ],
        compiler_params=pltpu.CompilerParams(
            collective_id=0, has_side_effects=True, vmem_limit_bytes=60 * 1024 * 1024
        ),
        cost_estimate=pl.CostEstimate(
            flops=6 * rows * width * hidden, bytes_accessed=8 * rows * width, transcendentals=0
        ),
    )(outgoing, gate_local, up_local, down_local)


def expert_collectives(outgoing, gate_local, up_local, down_local):
    experts, capacity, model_width = outgoing.shape
    received = lax.all_to_all(outgoing, "ep", split_axis=0, concat_axis=0, tiled=True)
    all_rows = lax.all_gather(received, "sp", axis=0, tiled=True).reshape(-1, model_width)
    gate_out = jnp.dot(all_rows, gate_local, preferred_element_type=jnp.float32)
    up_out = jnp.dot(all_rows, up_local, preferred_element_type=jnp.float32)
    activated = (jax.nn.silu(gate_out) * up_out).astype(jnp.bfloat16)
    summed = lax.psum_scatter(
        jnp.dot(activated, down_local, preferred_element_type=jnp.float32).astype(jnp.bfloat16),
        "sp",
        scatter_dimension=0,
        tiled=True,
    )
    expert_out = summed.reshape(experts, capacity, model_width)
    return lax.all_to_all(expert_out, "ep", split_axis=0, concat_axis=0, tiled=True)


def on_device(
    stream,
    query_base,
    key_heads,
    value_heads,
    attention_gain,
    expert_gain,
    adapter_down,
    adapter_up,
    user_index,
    routes,
    route_weights,
    gate_weight,
    up_weight,
    down_weight,
):
    user_id = user_index[0]
    tokens_dev, model_width = stream.shape
    down_cols = lax.dynamic_slice_in_dim(adapter_down, user_id * RANK, RANK, 1).T
    up_cols = lax.dynamic_slice_in_dim(adapter_up, user_id * RANK, RANK, 1).T
    shared = jnp.concatenate([key_heads, value_heads, down_cols, up_cols], axis=0)
    shared = lax.all_gather(shared, "sp", axis=0, tiled=False)
    key_all = shared[:, :tokens_dev].reshape(-1, key_heads.shape[1])
    value_all = shared[:, tokens_dev : 2 * tokens_dev].reshape(-1, value_heads.shape[1])
    adapters = shared[:, 2 * tokens_dev :].transpose(1, 0, 2).reshape(2 * RANK, model_width)
    hidden_state = attention_block(
        stream, query_base, key_all, value_all, attention_gain, adapters[:RANK], adapters[RANK:]
    )
    normed_moe = rms_scale(hidden_state, expert_gain).astype(jnp.bfloat16)
    top_count = routes.shape[1]
    experts = lax.axis_size("ep")
    capacity = max(2, (5 * tokens_dev * top_count + 4 * experts - 1) // (4 * experts))
    own_routes = lax.dynamic_slice_in_dim(routes, lax.axis_index("sp") * tokens_dev, tokens_dev, 0)
    in_kernel = experts == STEPS and capacity % 8 == 0 and lax.axis_size("sp") == 4
    flat_routes, slot_index = route_slots(own_routes, experts)
    if in_kernel:
        mask = flat_routes ^ lax.axis_index("ep")
        near, far = (mask // 2) % 2, mask // 4
        flat_routes = mask % 2 + 4 * near + 2 * ((far + near) % 2)
    position = (flat_routes * capacity + slot_index).reshape(tokens_dev, top_count)
    slots = jnp.arange(experts * capacity, dtype=jnp.int32)
    chosen = position[:, :, None] == slots
    placed = jnp.any(chosen, axis=1).astype(jnp.bfloat16)
    outgoing = (
        lax.dot_general(
            placed, normed_moe, (((0,), (0,)), ((), ())), preferred_element_type=jnp.float32
        )
        .astype(jnp.bfloat16)
        .reshape(experts, capacity, model_width)
    )
    exchange = expert_exchange if in_kernel else expert_collectives
    returned = exchange(outgoing, gate_weight[0], up_weight[0], down_weight[0])
    returned = returned.reshape(experts * capacity, model_width)
    route_share = route_weights.astype(jnp.float32)
    route_share = route_share / jnp.sum(route_share, axis=1, keepdims=True)
    moe_out = sum(
        jnp.dot(
            chosen[:, k].astype(jnp.bfloat16), returned, preferred_element_type=jnp.float32
        )
        * route_share[:, k : k + 1]
        for k in range(top_count)
    ).astype(jnp.bfloat16)
    return (hidden_state, moe_out)


def solution(mesh):
    in_specs = (
        P(("ep", "sp"), None),
        P(("ep", "sp"), None),
        P(("ep", "sp"), None),
        P(("ep", "sp"), None),
        P(),
        P(),
        P("sp", None),
        P("sp", None),
        P("ep"),
        P("ep", None),
        P(("ep", "sp"), None),
        P("ep", None, "sp"),
        P("ep", None, "sp"),
        P("ep", "sp", None),
    )
    out_specs = (P(("ep", "sp"), None), P(("ep", "sp"), None))
    return jax.shard_map(
        on_device, mesh=mesh, in_specs=in_specs, out_specs=out_specs, check_vma=False
    )
```
